32 devices in a mesh: chan: 4 (over y, core), tm: 8 (over z, x).
Axes of the slice: x: 2, y: 2, z: 4, core: 2. Of those that a mesh axis runs over, the one named last changes fastest.
Arguments:
- record: bfloat16 [2048, 16, 2560], P('chan', 'tm'), may hold values from -6 to 6
- partners: int32 [2048, 8], P('chan'), may hold values from 0 to 2047, as said below
- block_owner: int32 [4, 8], P('chan'), may hold values from 0 to 7, each once within a row
Outputs:
- stacks: float32 [16384, 257], P(('chan', 'tm'))
The draws below stay inside these ranges and needn't reach their ends.
Inputs may be any that keep to these rules, and one draw needn't show every extreme that they name: `partners`: every partner is another channel at most 512 channels away; in every channel block one channel has a partner exactly 512 away. `block_owner`: each row names every index of tm once.
All inputs are finite; a program needn't handle non-finite values.
Results may differ from the reference program's by a relative error of at most 0.0028.
Values may be sent and summed in bfloat16 or wider, within the bound.
A program may use at most 128 MiB of HBM per device.

```python
import math
import jax
import jax.numpy as jnp
from jax import lax

CB = 512
L = 2560
NFB = 512
F0 = 64
K = 8
LAG = 128
SPAN = 512
C = 2048
WINDOWS = 16
NLAG = 257
PADDED = 5120
N_CHAN = 4
N_TM = 8


def draw_record(key, part):
    key_common, key_incoherent = jax.random.split(jax.random.fold_in(key, 23))
    lead_room = N_CHAN * LAG
    common = jax.random.normal(key_common, (WINDOWS, L + lead_room), jnp.float32)
    incoherent = jax.random.normal(key_incoherent, (C, WINDOWS, L), jnp.float32)
    channel = jnp.arange(C, dtype=jnp.int32)[:, None]
    sample_time = jnp.arange(L, dtype=jnp.int32)[None, :]
    sample_index = sample_time + lead_room - channel * LAG // SPAN

    def delayed(series):
        return jnp.take(series, sample_index, axis=0)
    coherent = jax.vmap(delayed, in_axes=0, out_axes=1)(common)
    summed = 0.9 * coherent + 0.45 * incoherent
    return jnp.clip(summed, -6.0, 6.0).astype(jnp.bfloat16)


def draw_partners(key, part):
    key_dist, key_side, key_pick = jax.random.split(jax.random.fold_in(key, 11), 3)
    channel = jnp.arange(C, dtype=jnp.int32)[:, None]
    distance = jax.random.randint(key_dist, (C, K), 1, SPAN + 1, dtype=jnp.int32)
    direction = jax.random.randint(key_side, (C, K), 0, 2, dtype=jnp.int32) * 2 - 1
    offsets = distance * direction
    target = channel + offsets
    outside = (target < 0) | (target >= C)
    target = jnp.where(outside, channel - offsets, target)
    picked = jax.random.randint(key_pick, (N_CHAN,), 0, CB, dtype=jnp.int32)
    flat = channel[:, 0]
    chosen = flat % CB == picked[flat // CB]
    farthest = jnp.where(flat + SPAN < C, flat + SPAN, flat - SPAN)
    slot_zero = jnp.where(chosen, farthest, target[:, 0])
    return jnp.concatenate([slot_zero[:, None], target[:, 1:]], axis=1).astype(jnp.int32)


def setup_inputs(seed: int = 0) -> dict:
    key_of = jax.random.split(jax.random.key(seed), 4)
    return {
        "record": draw_record(jax.random.fold_in(key_of[3], 71), 0),
        "partners": draw_partners(jax.random.fold_in(key_of[3], 71), 0),
        "block_owner": jax.vmap(lambda own: jax.random.permutation(own, N_TM))(jax.random.split(key_of[2], N_CHAN)).reshape((N_CHAN, N_TM)).astype(jnp.int32),
    }


def fourier_table():
    times = jnp.arange(L, dtype=jnp.int32)[:, None]
    freqs = (F0 + jnp.arange(NFB, dtype=jnp.int32))[None, :]
    phase = (times * freqs % PADDED).astype(jnp.float32) * (2.0 * math.pi / PADDED)
    return jnp.concatenate([jnp.cos(phase), -jnp.sin(phase)], axis=1).astype(jnp.bfloat16)

def lag_table():
    freqs = (F0 + jnp.arange(NFB, dtype=jnp.int32))[:, None]
    shifts = (jnp.arange(NLAG, dtype=jnp.int32) - LAG)[None, :]
    phase = (freqs * shifts % PADDED).astype(jnp.float32) * (2.0 * math.pi / PADDED)
    return jnp.concatenate([jnp.cos(phase), -jnp.sin(phase)], axis=0)

def whiten(rows, fourier):
    flat = rows.reshape(-1, L)
    spectra = jnp.dot(flat, fourier, preferred_element_type=jnp.float32)
    real_part = spectra[:, :NFB]
    imag_part = spectra[:, NFB:]
    energy = real_part * real_part + imag_part * imag_part
    level = lax.optimization_barrier(jnp.mean(energy, axis=1, keepdims=True))
    divisor = jnp.sqrt(energy + 0.1 * level + 1e-05)
    whitened = jnp.concatenate([real_part / divisor, imag_part / divisor], axis=1)
    return whitened.astype(jnp.bfloat16).reshape(rows.shape[0], rows.shape[1], 2 * NFB)

def cross_spectra(own_rows, partner_rows):
    own_real = own_rows[:, None, :, :NFB].astype(jnp.float32)
    own_imag = own_rows[:, None, :, NFB:].astype(jnp.float32)
    far_real = partner_rows[:, :, :, :NFB].astype(jnp.float32)
    far_imag = partner_rows[:, :, :, NFB:].astype(jnp.float32)
    cross_real = lax.optimization_barrier(jnp.sum(own_real * far_real + own_imag * far_imag, axis=2))
    cross_imag = lax.optimization_barrier(jnp.sum(own_real * far_imag - own_imag * far_real, axis=2))
    joined = jnp.concatenate([cross_real, cross_imag], axis=2)
    return joined.reshape(-1, 2 * NFB)

def reference(record, partners, block_owner):
    fourier = fourier_table()
    blocks = record.reshape(N_CHAN, CB, WINDOWS, L)
    whitened = lax.map(lambda rows: whiten(rows, fourier), blocks).reshape(C, WINDOWS, 2 * NFB)
    own_blocks = whitened.reshape(N_CHAN, CB, WINDOWS, 2 * NFB)
    partner_blocks = partners.reshape(N_CHAN, CB, K)

    def one_block(inputs):
        own_rows, indices = inputs
        return cross_spectra(own_rows, jnp.take(whitened, indices.astype(jnp.int32), axis=0))
    cross = lax.map(one_block, (own_blocks, partner_blocks)).reshape(C * K, 2 * NFB)
    scale = 1.0 / math.sqrt(WINDOWS * NFB)
    lags = jnp.dot(cross, lag_table(), precision=lax.Precision.HIGHEST, preferred_element_type=jnp.float32) * scale
    lags = lags.reshape(N_CHAN, N_TM, CB * K // N_TM, NLAG)
    inverse = jnp.argsort(block_owner, axis=1).astype(jnp.int32)
    placed = jnp.take_along_axis(lags, inverse[:, :, None, None], axis=1)
    return placed.reshape(C * K, NLAG)
```

```python
import functools
import math

import jax
import jax.numpy as jnp
import ml_dtypes
import numpy as np
from jax import lax
from jax.experimental import pallas as pl
from jax.experimental.pallas import tpu as pltpu
from jax.sharding import PartitionSpec as P

NFB = 512
F0 = 64
K = 8
LAG = 128
CHUNKS = 2
MESH = pl.DeviceIdType.MESH


def split(table):
    high = table.astype(ml_dtypes.bfloat16)
    low = (table - high.astype(np.float64)).astype(ml_dtypes.bfloat16)
    return high, low


def tables(samples):
    freqs = F0 + np.arange(NFB, dtype=np.int64)
    turn = 2.0 * math.pi / (2 * samples)
    angle = np.arange(samples, dtype=np.int64)[:, None] * freqs[None, :] % (2 * samples) * turn
    fourier = np.concatenate([np.cos(angle), -np.sin(angle)], axis=1).astype(ml_dtypes.bfloat16)
    shift = np.arange(LAG + 1, dtype=np.int64)[None, :]
    phi = freqs[:, None] * shift % (2 * samples) * turn
    cos_high, cos_low = split(np.cos(phi))
    sin_high, sin_low = split(np.sin(phi))
    cosine = np.concatenate([cos_high[:, :LAG], cos_low[:, :LAG]], axis=1)
    order = np.concatenate([[LAG], np.arange(1, LAG)])
    sine = np.concatenate([sin_high[:, order], sin_low[:, order]], axis=1)
    last = np.concatenate([np.tile(cos_high[:, LAG], (8, 1)), np.tile(cos_low[:, LAG], (8, 1))])
    return fourier, cosine, sine, last


def kernel(n_chan, n_tm, scale, rows_ref, owner_ref, x_hbm, f_hbm, cos_ref, sin_ref, last_ref, out_ref,
           x, table, spread, white, cr, ci, send, recv,
           load_sem, halo_send, halo_recv, lag_send, lag_recv):
    windows, block, samples = x.shape
    chan, me = lax.axis_index("chan"), lax.axis_index("tm")
    has_left, has_right = chan > 0, chan < n_chan - 1
    part = block // CHUNKS
    pairs = out_ref.shape[0]
    channels = pairs // K

    table_copy = pltpu.make_async_copy(f_hbm, table, load_sem.at[CHUNKS])
    loads = [
        pltpu.make_async_copy(
            x_hbm.at[:, pl.ds(c * part, part), :], x.at[:, pl.ds(c * part, part), :], load_sem.at[c]
        )
        for c in range(CHUNKS)
    ]
    loads[0].start()
    table_copy.start()
    for c in range(1, CHUNKS):
        loads[c].start()

    barrier = pltpu.get_barrier_semaphore()
    for s in range(1, n_tm):
        pl.semaphore_signal(barrier, inc=1, device_id=(chan, lax.rem(me + s, n_tm)), device_id_type=MESH)

    @pl.when(has_left)
    def _():
        pl.semaphore_signal(barrier, inc=1, device_id=(chan - 1, me), device_id_type=MESH)

    @pl.when(has_right)
    def _():
        pl.semaphore_signal(barrier, inc=1, device_id=(chan + 1, me), device_id_type=MESH)

    def halo(c, side):
        start = 2 * block if side == 0 else 0
        return pltpu.make_async_remote_copy(
            src_ref=white.at[pl.ds(block + c * part, part)],
            dst_ref=white.at[pl.ds(start + c * part, part)],
            send_sem=halo_send.at[side, c],
            recv_sem=halo_recv.at[side, c],
            device_id=(chan - 1 if side == 0 else chan + 1, me),
            device_id_type=MESH,
        )

    for c in range(CHUNKS):
        loads[c].wait()
        if c == 0:
            table_copy.wait()
        for w in range(windows):
            spectra = jnp.dot(x[w, c * part:(c + 1) * part, :], table[...], preferred_element_type=jnp.float32)
            real, imag = spectra[:, :NFB], spectra[:, NFB:]
            energy = real * real + imag * imag
            level = jnp.sum(energy, axis=1, keepdims=True) * (1.0 / NFB)
            factor = lax.rsqrt(energy + 0.1 * level + 1e-05)
            real, imag = real * factor, imag * factor
            for q in range(4):
                lanes = slice(q * 128, (q + 1) * 128)
                spread[pl.ds(w * 4 + q, part, stride=16), :] = real[:, lanes]
                spread[pl.ds(8 + w * 4 + q, part, stride=16), :] = imag[:, lanes]

        def pack(i, carry):
            tile = spread[pl.ds(pl.multiple_of(i * 256, 256), 256), :].reshape(16, 16, 128)
            white[pl.ds(block + c * part + i * 16, 16)] = tile.astype(jnp.bfloat16)
            return carry

        lax.fori_loop(0, part // 16, pack, 0)
        if c == 0:
            pl.semaphore_wait(barrier, n_tm - 1 + has_left.astype(jnp.int32) + has_right.astype(jnp.int32))

        @pl.when(has_left)
        def _():
            halo(c, 0).start()

        @pl.when(has_right)
        def _():
            halo(c, 1).start()

    @pl.when(has_left)
    def _():
        for c in range(CHUNKS):
            halo(c, 0).wait_send()
            halo(c, 1).wait_recv()

    @pl.when(has_right)
    def _():
        for c in range(CHUNKS):
            halo(c, 1).wait_send()
            halo(c, 0).wait_recv()

    def lag_copy(s):
        return pltpu.make_async_remote_copy(
            src_ref=send.at[s - 1],
            dst_ref=recv.at[s - 1],
            send_sem=lag_send.at[s - 1],
            recv_sem=lag_recv.at[s - 1],
            device_id=(chan, lax.rem(me + s, n_tm)),
            device_id_type=MESH,
        )

    def pair_block(s, carry):
        first = owner_ref[lax.rem(me + s, n_tm)] * channels

        def one_channel(i, inner):
            row = first + i
            own = white[block + row].astype(jnp.float32)
            own_real, own_imag = own[:8], own[8:]
            for k in range(K):
                far = white[rows_ref[row * K + k]].astype(jnp.float32)
                far_real, far_imag = far[:8], far[8:]
                at = pl.ds(pl.multiple_of(i * (8 * K) + 8 * k, 8), 8)
                cr[at, :] = own_real * far_real + own_imag * far_imag
                ci[at, :] = own_real * far_imag - own_imag * far_real
            return inner

        lax.fori_loop(0, channels, one_channel, 0, unroll=2)

        def gathered(ref):
            return jnp.concatenate(
                [
                    (ref[pl.ds(q, pairs, stride=8), :] + ref[pl.ds(q + 4, pairs, stride=8), :]).astype(jnp.bfloat16)
                    for q in range(4)
                ],
                axis=1,
            )

        real = gathered(cr)
        even = jnp.dot(real, cos_ref[...], preferred_element_type=jnp.float32)
        odd = jnp.dot(gathered(ci), sin_ref[...], preferred_element_type=jnp.float32)
        send[s - 1, :pairs, :LAG] = (even[:, :LAG] + even[:, LAG:]).astype(jnp.bfloat16)
        send[s - 1, :pairs, LAG:] = (odd[:, :LAG] + odd[:, LAG:]).astype(jnp.bfloat16)
        edge = lax.dot_general(
            last_ref[...], real, (((1,), (1,)), ((), ())), preferred_element_type=jnp.float32
        )
        edge = edge[:8] + edge[8:]
        pieces = [edge[:, q * 256:(q + 1) * 256] for q in range(pairs // 256)]
        send[s - 1, pairs:, :] = jnp.concatenate(pieces * (2 // len(pieces)), axis=0).astype(jnp.bfloat16)

        @pl.when(s < n_tm)
        def _():
            lag_copy(s).start()

        return carry

    lax.fori_loop(1, n_tm + 1, pair_block, 0)

    for s in range(1, n_tm):
        lag_copy(s).wait_recv()

    sub = lax.broadcasted_iota(jnp.int32, (128, 128), 0)
    lane = lax.broadcasted_iota(jnp.int32, (128, 128), 1)
    flip = jnp.where(sub + lane == LAG, 1.0, 0.0).astype(jnp.float32)

    def summed(rows):
        total = send[n_tm - 1, rows, :].astype(jnp.float32)
        for s in range(1, n_tm):
            total = total + recv[s - 1, rows, :].astype(jnp.float32)
        return total * scale

    edges = summed(slice(pairs, pairs + 16))
    for c in range(pairs // 128):
        total = summed(slice(c * 128, (c + 1) * 128))
        even, odd = total[:, :LAG], total[:, LAG:]
        at = c * 128 // 256 * 8
        edge = jnp.broadcast_to(edges[at:at + 1, c * 128 % 256:c * 128 % 256 + 128], (128, 128)).T
        odd_edge = odd[:, 0:1]
        odd = jnp.where(lane == 0, 0.0, odd)
        left = jnp.dot(
            even + odd, flip, precision=lax.Precision.HIGHEST, preferred_element_type=jnp.float32
        )
        rows = slice(c * 128, (c + 1) * 128)
        out_ref[rows, :LAG] = jnp.where(lane == 0, edge + odd_edge, left)
        out_ref[rows, LAG:2 * LAG] = even - odd
        out_ref[rows, 2 * LAG:] = edge[:, 0:1] - odd_edge

    for s in range(1, n_tm):
        lag_copy(s).wait_send()


def shards(n_chan, n_tm, constants, record, partners, block_owner):
    block, windows, samples = record.shape
    pairs = block * K // n_tm
    base = lax.axis_index("chan") * block - block
    rows = (partners - base).reshape(-1)
    count = jnp.arange(n_tm, dtype=jnp.int32)
    onehot = (block_owner[0][None, :] == count[:, None]).astype(jnp.int32)
    inverse = jnp.sum(onehot * count[None, :], axis=1)
    scale = 1.0 / math.sqrt(windows * n_tm * NFB)
    smem = pl.BlockSpec(memory_space=pltpu.SMEM)
    vmem = pl.BlockSpec(memory_space=pltpu.VMEM)
    anywhere = pl.BlockSpec(memory_space=pl.ANY)
    return pl.pallas_call(
        functools.partial(kernel, n_chan, n_tm, scale),
        out_shape=jax.ShapeDtypeStruct((pairs, 2 * LAG + 1), jnp.float32),
        in_specs=[smem, smem, anywhere, anywhere, vmem, vmem, vmem],
        out_specs=vmem,
        scratch_shapes=[
            pltpu.VMEM((windows, block, samples), jnp.bfloat16),
            pltpu.VMEM((samples, 2 * NFB), jnp.bfloat16),
            pltpu.VMEM((block // CHUNKS * 16, 128), jnp.float32),
            pltpu.VMEM((3 * block, 16, 128), jnp.bfloat16),
            pltpu.VMEM((pairs * 8, 128), jnp.float32),
            pltpu.VMEM((pairs * 8, 128), jnp.float32),
            pltpu.VMEM((n_tm, pairs + 16, 2 * LAG), jnp.bfloat16),
            pltpu.VMEM((n_tm - 1, pairs + 16, 2 * LAG), jnp.bfloat16),
            pltpu.SemaphoreType.DMA((CHUNKS + 1,)),
            pltpu.SemaphoreType.DMA((2, CHUNKS)),
            pltpu.SemaphoreType.DMA((2, CHUNKS)),
            pltpu.SemaphoreType.DMA((n_tm - 1,)),
            pltpu.SemaphoreType.DMA((n_tm - 1,)),
        ],
        compiler_params=pltpu.CompilerParams(
            collective_id=0, has_side_effects=True, vmem_limit_bytes=52 * 1024 * 1024
        ),
        cost_estimate=pl.CostEstimate(
            flops=2 * block * windows * samples * 2 * NFB, bytes_accessed=16 * 1024 * 1024, transcendentals=0
        ),
    )(rows, inverse, jnp.transpose(record, (1, 0, 2)), *(jnp.asarray(c) for c in constants))


def solution(mesh):
    placed = (P("chan", "tm", None), P("chan", None), P("chan", None))

    def run(record, partners, block_owner):
        body = functools.partial(shards, mesh.shape["chan"], mesh.shape["tm"], tables(record.shape[2]))
        return jax.shard_map(
            body, mesh=mesh, in_specs=placed, out_specs=P(("chan", "tm"), None), check_vma=False
        )(record, partners, block_owner)

    return run
```

```python
import functools
import math

import jax
import jax.numpy as jnp
import ml_dtypes
import numpy as np
from jax import lax
from jax.experimental import pallas as pl
from jax.experimental.pallas import tpu as pltpu
from jax.sharding import PartitionSpec as P

NFB = 512
F0 = 64
K = 8
LAG = 128
CHUNKS = 2
MESH = pl.DeviceIdType.MESH


def split(table):
    high = table.astype(ml_dtypes.bfloat16)
    low = (table - high.astype(np.float64)).astype(ml_dtypes.bfloat16)
    return high, low


def tables(samples):
    freqs = F0 + np.arange(NFB, dtype=np.int64)
    turn = 2.0 * math.pi / (2 * samples)
    angle = np.arange(samples, dtype=np.int64)[:, None] * freqs[None, :] % (2 * samples) * turn
    fourier = np.concatenate([np.cos(angle), -np.sin(angle)], axis=1).astype(ml_dtypes.bfloat16)
    shift = np.arange(LAG + 1, dtype=np.int64)[None, :]
    phi = freqs[:, None] * shift % (2 * samples) * turn
    cos_high, cos_low = split(np.cos(phi))
    sin_high, sin_low = split(np.sin(phi))
    cosine = np.concatenate([cos_high[:, :LAG], cos_low[:, :LAG]], axis=1)
    order = np.concatenate([[LAG], np.arange(1, LAG)])
    sine = np.concatenate([sin_high[:, order], sin_low[:, order]], axis=1)
    last = np.concatenate([np.tile(cos_high[:, LAG], (8, 1)), np.tile(cos_low[:, LAG], (8, 1))])
    return fourier, cosine, sine, last


def kernel(n_chan, n_tm, scale, rows_ref, owner_ref, x_hbm, f_hbm, cos_ref, sin_ref, last_ref, out_ref,
           x, table, spread, white, cr, ci, send, recv,
           load_sem, halo_send, halo_recv, lag_send, lag_recv):
    windows, block, samples = x.shape
    chan, me = lax.axis_index("chan"), lax.axis_index("tm")
    has_left, has_right = chan > 0, chan < n_chan - 1
    part = block // CHUNKS
    pairs = out_ref.shape[0]
    channels = pairs // K

    table_copy = pltpu.make_async_copy(f_hbm, table, load_sem.at[CHUNKS])
    loads = [
        pltpu.make_async_copy(
            x_hbm.at[:, pl.ds(c * part, part), :], x.at[:, pl.ds(c * part, part), :], load_sem.at[c]
        )
        for c in range(CHUNKS)
    ]
    loads[0].start()
    table_copy.start()
    for c in range(1, CHUNKS):
        loads[c].start()

    barrier = pltpu.get_barrier_semaphore()
    for s in range(1, n_tm):
        pl.semaphore_signal(barrier, inc=1, device_id=(chan, lax.rem(me + s, n_tm)), device_id_type=MESH)

    @pl.when(has_left)
    def _():
        pl.semaphore_signal(barrier, inc=1, device_id=(chan - 1, me), device_id_type=MESH)

    @pl.when(has_right)
    def _():
        pl.semaphore_signal(barrier, inc=1, device_id=(chan + 1, me), device_id_type=MESH)

    def halo(c, side):
        start = 2 * block if side == 0 else 0
        return pltpu.make_async_remote_copy(
            src_ref=white.at[pl.ds(block + c * part, part)],
            dst_ref=white.at[pl.ds(start + c * part, part)],
            send_sem=halo_send.at[side, c],
            recv_sem=halo_recv.at[side, c],
            device_id=(chan - 1 if side == 0 else chan + 1, me),
            device_id_type=MESH,
        )

    for c in range(CHUNKS):
        loads[c].wait()
        if c == 0:
            table_copy.wait()
        for w in range(windows):
            spectra = jnp.dot(x[w, c * part:(c + 1) * part, :], table[...], preferred_element_type=jnp.float32)
            real, imag = spectra[:, :NFB], spectra[:, NFB:]
            energy = real * real + imag * imag
            level = jnp.sum(energy, axis=1, keepdims=True) * (1.0 / NFB)
            factor = lax.rsqrt(energy + 0.1 * level + 1e-05)
            real, imag = real * factor, imag * factor
            for q in range(4):
                lanes = slice(q * 128, (q + 1) * 128)
                spread[pl.ds(w * 4 + q, part, stride=16), :] = real[:, lanes]
                spread[pl.ds(8 + w * 4 + q, part, stride=16), :] = imag[:, lanes]

        def pack(i, carry):
            tile = spread[pl.ds(pl.multiple_of(i * 256, 256), 256), :].reshape(16, 16, 128)
            white[pl.ds(block + c * part + i * 16, 16)] = tile.astype(jnp.bfloat16)
            return carry

        lax.fori_loop(0, part // 16, pack, 0)
        if c == 0:
            pl.semaphore_wait(barrier, n_tm - 1 + has_left.astype(jnp.int32) + has_right.astype(jnp.int32))

        @pl.when(has_left)
        def _():
            halo(c, 0).start()

        @pl.when(has_right)
        def _():
            halo(c, 1).start()

    @pl.when(has_left)
    def _():
        for c in range(CHUNKS):
            halo(c, 0).wait_send()
            halo(c, 1).wait_recv()

    @pl.when(has_right)
    def _():
        for c in range(CHUNKS):
            halo(c, 1).wait_send()
            halo(c, 0).wait_recv()

    def lag_copy(s):
        return pltpu.make_async_remote_copy(
            src_ref=send.at[s - 1],
            dst_ref=recv.at[s - 1],
            send_sem=lag_send.at[s - 1],
            recv_sem=lag_recv.at[s - 1],
            device_id=(chan, lax.rem(me + s, n_tm)),
            device_id_type=MESH,
        )

    base = chan * block - block
    upper = lax.broadcasted_iota(jnp.int32, (8, 128), 0) < 4

    def both_windows(first, second):
        return jnp.where(upper, first, second) + pltpu.roll(jnp.where(upper, second, first), 4, 0)

    def pair_block(s, carry):
        target = lax.rem(me + s, n_tm)
        first = jnp.int32(0)
        for j in range(n_tm):
            first = jnp.where(owner_ref[0, j] == target, j * channels, first)

        def one_channel(i, inner):
            row = first + i
            own = white[block + row].astype(jnp.float32)
            own_real, own_imag = own[:8], own[8:]
            for k in range(0, K, 2):
                real, imag = [], []
                for far_slot in (k, k + 1):
                    far = white[jnp.maximum(rows_ref[far_slot, row] - base, 0)].astype(jnp.float32)
                    far_real, far_imag = far[:8], far[8:]
                    real.append(own_real * far_real + own_imag * far_imag)
                    imag.append(own_real * far_imag - own_imag * far_real)
                at = pl.ds(pl.multiple_of(i * (4 * K) + 4 * k, 8), 8)
                cr[at, :] = both_windows(*real)
                ci[at, :] = both_windows(*imag)
            return inner

        lax.fori_loop(0, channels, one_channel, 0, unroll=4)

        def gathered(ref):
            return jnp.concatenate(
                [
                    ref[pl.ds(q, pairs, stride=4), :].astype(jnp.bfloat16)
                    for q in range(4)
                ],
                axis=1,
            )

        real = gathered(cr)
        even = jnp.dot(real, cos_ref[...], preferred_element_type=jnp.float32)
        odd = jnp.dot(gathered(ci), sin_ref[...], preferred_element_type=jnp.float32)
        send[s - 1, :pairs, :LAG] = (even[:, :LAG] + even[:, LAG:]).astype(jnp.bfloat16)
        send[s - 1, :pairs, LAG:] = (odd[:, :LAG] + odd[:, LAG:]).astype(jnp.bfloat16)
        edge = lax.dot_general(
            last_ref[...], real, (((1,), (1,)), ((), ())), preferred_element_type=jnp.float32
        )
        edge = edge[:8] + edge[8:]
        pieces = [edge[:, q * 256:(q + 1) * 256] for q in range(pairs // 256)]
        send[s - 1, pairs:, :] = jnp.concatenate(pieces * (2 // len(pieces)), axis=0).astype(jnp.bfloat16)

        @pl.when(s < n_tm)
        def _():
            lag_copy(s).start()

        return carry

    lax.fori_loop(1, n_tm + 1, pair_block, 0)

    for s in range(1, n_tm):
        lag_copy(s).wait_recv()

    sub = lax.broadcasted_iota(jnp.int32, (128, 128), 0)
    lane = lax.broadcasted_iota(jnp.int32, (128, 128), 1)
    flip = jnp.where(sub + lane == LAG, 1.0, 0.0).astype(jnp.float32)

    def summed(rows):
        total = send[n_tm - 1, rows, :].astype(jnp.float32)
        for s in range(1, n_tm):
            total = total + recv[s - 1, rows, :].astype(jnp.float32)
        return total * scale

    edges = summed(slice(pairs, pairs + 16))
    for c in range(pairs // 128):
        total = summed(slice(c * 128, (c + 1) * 128))
        even, odd = total[:, :LAG], total[:, LAG:]
        at = c * 128 // 256 * 8
        edge = jnp.broadcast_to(edges[at:at + 1, c * 128 % 256:c * 128 % 256 + 128], (128, 128)).T
        odd_edge = odd[:, 0:1]
        odd = jnp.where(lane == 0, 0.0, odd)
        left = jnp.dot(
            even + odd, flip, precision=lax.Precision.HIGHEST, preferred_element_type=jnp.float32
        )
        rows = slice(c * 128, (c + 1) * 128)
        out_ref[rows, :LAG] = jnp.where(lane == 0, edge + odd_edge, left)
        out_ref[rows, LAG:2 * LAG] = even - odd
        out_ref[rows, 2 * LAG:] = edge[:, 0:1] - odd_edge

    for s in range(1, n_tm):
        lag_copy(s).wait_send()


def shards(n_chan, n_tm, constants, record, partners, block_owner):
    block, windows, samples = record.shape
    pairs = block * K // n_tm
    scale = 1.0 / math.sqrt(windows * n_tm * NFB)
    smem = pl.BlockSpec(memory_space=pltpu.SMEM)
    vmem = pl.BlockSpec(memory_space=pltpu.VMEM)
    anywhere = pl.BlockSpec(memory_space=pl.ANY)
    return pl.pallas_call(
        functools.partial(kernel, n_chan, n_tm, scale),
        out_shape=jax.ShapeDtypeStruct((pairs, 2 * LAG + 1), jnp.float32),
        in_specs=[smem, smem, anywhere, anywhere, vmem, vmem, vmem],
        out_specs=vmem,
        scratch_shapes=[
            pltpu.VMEM((windows, block, samples), jnp.bfloat16),
            pltpu.VMEM((samples, 2 * NFB), jnp.bfloat16),
            pltpu.VMEM((block // CHUNKS * 16, 128), jnp.float32),
            pltpu.VMEM((3 * block, 16, 128), jnp.bfloat16),
            pltpu.VMEM((pairs * 4, 128), jnp.float32),
            pltpu.VMEM((pairs * 4, 128), jnp.float32),
            pltpu.VMEM((n_tm, pairs + 16, 2 * LAG), jnp.bfloat16),
            pltpu.VMEM((n_tm - 1, pairs + 16, 2 * LAG), jnp.bfloat16),
            pltpu.SemaphoreType.DMA((CHUNKS + 1,)),
            pltpu.SemaphoreType.DMA((2, CHUNKS)),
            pltpu.SemaphoreType.DMA((2, CHUNKS)),
            pltpu.SemaphoreType.DMA((n_tm - 1,)),
            pltpu.SemaphoreType.DMA((n_tm - 1,)),
        ],
        compiler_params=pltpu.CompilerParams(
            collective_id=0, has_side_effects=True, vmem_limit_bytes=52 * 1024 * 1024
        ),
        cost_estimate=pl.CostEstimate(
            flops=2 * block * windows * samples * 2 * NFB, bytes_accessed=16 * 1024 * 1024, transcendentals=0
        ),
    )(jnp.transpose(partners), block_owner, jnp.transpose(record, (1, 0, 2)), *(jnp.asarray(c) for c in constants))


def solution(mesh):
    placed = (P("chan", "tm", None), P("chan", None), P("chan", None))

    def run(record, partners, block_owner):
        body = functools.partial(shards, mesh.shape["chan"], mesh.shape["tm"], tables(record.shape[2]))
        return jax.shard_map(
            body, mesh=mesh, in_specs=placed, out_specs=P(("chan", "tm"), None), check_vma=False
        )(record, partners, block_owner)

    return run
```

```python
import functools
import math

import jax
import jax.numpy as jnp
import ml_dtypes
import numpy as np
from jax import lax
from jax.experimental import pallas as pl
from jax.experimental.pallas import tpu as pltpu
from jax.sharding import PartitionSpec as P

NFB = 512
F0 = 64
K = 8
LAG = 128
CHUNKS = 2
MESH = pl.DeviceIdType.MESH


def split(table):
    high = table.astype(ml_dtypes.bfloat16)
    low = (table - high.astype(np.float64)).astype(ml_dtypes.bfloat16)
    return high, low


def tables(samples):
    freqs = F0 + np.arange(NFB, dtype=np.int64)
    turn = 2.0 * math.pi / (2 * samples)
    angle = np.arange(samples, dtype=np.int64)[:, None] * freqs[None, :] % (2 * samples) * turn
    fourier = np.concatenate([np.cos(angle), -np.sin(angle)], axis=1).astype(ml_dtypes.bfloat16)
    shift = np.arange(LAG + 1, dtype=np.int64)[None, :]
    phi = freqs[:, None] * shift % (2 * samples) * turn
    cos_high, cos_low = split(np.cos(phi))
    sin_high, sin_low = split(np.sin(phi))
    cosine = np.concatenate([cos_high[:, :LAG], cos_low[:, :LAG]], axis=1)
    order = np.concatenate([[LAG], np.arange(1, LAG)])
    sine = np.concatenate([sin_high[:, order], sin_low[:, order]], axis=1)
    last = np.concatenate([np.tile(cos_high[:, LAG], (8, 1)), np.tile(cos_low[:, LAG], (8, 1))])
    return fourier, cosine, sine, last


def kernel(n_chan, n_tm, scale, rows_ref, owner_ref, x_hbm, f_hbm, cos_ref, sin_ref, last_ref, out_ref,
           x, table, spread, white, cr, ci, mine, fold_out, fold_in, send, recv,
           load_sem, halo_send, halo_recv, fold_send, fold_recv, lag_send, lag_recv):
    windows, block, samples = x.shape
    chan, me = lax.axis_index("chan"), lax.axis_index("tm")
    half = n_tm // 2
    side = lax.rem(me, 2)
    mate = me + 1 - 2 * side
    has_left, has_right = chan > 0, chan < n_chan - 1
    part = block // CHUNKS
    pairs = out_ref.shape[0]
    channels = pairs // K

    table_copy = pltpu.make_async_copy(f_hbm, table, load_sem.at[CHUNKS])
    loads = [
        pltpu.make_async_copy(
            x_hbm.at[:, pl.ds(c * part, part), :], x.at[:, pl.ds(c * part, part), :], load_sem.at[c]
        )
        for c in range(CHUNKS)
    ]
    loads[0].start()
    table_copy.start()
    for c in range(1, CHUNKS):
        loads[c].start()

    barrier = pltpu.get_barrier_semaphore()
    pl.semaphore_signal(barrier, inc=1, device_id=(chan, mate), device_id_type=MESH)
    for s in range(1, half):
        pl.semaphore_signal(barrier, inc=1, device_id=(chan, lax.rem(me + 2 * s, n_tm)), device_id_type=MESH)

    @pl.when(has_left)
    def _():
        pl.semaphore_signal(barrier, inc=1, device_id=(chan - 1, me), device_id_type=MESH)

    @pl.when(has_right)
    def _():
        pl.semaphore_signal(barrier, inc=1, device_id=(chan + 1, me), device_id_type=MESH)

    def halo(c, way):
        start = 2 * block if way == 0 else 0
        return pltpu.make_async_remote_copy(
            src_ref=white.at[pl.ds(block + c * part, part)],
            dst_ref=white.at[pl.ds(start + c * part, part)],
            send_sem=halo_send.at[way, c],
            recv_sem=halo_recv.at[way, c],
            device_id=(chan - 1 if way == 0 else chan + 1, me),
            device_id_type=MESH,
        )

    for c in range(CHUNKS):
        loads[c].wait()
        if c == 0:
            table_copy.wait()
        for w in range(windows):
            spectra = jnp.dot(x[w, c * part:(c + 1) * part, :], table[...], preferred_element_type=jnp.float32)
            real, imag = spectra[:, :NFB], spectra[:, NFB:]
            energy = real * real + imag * imag
            level = jnp.sum(energy, axis=1, keepdims=True) * (1.0 / NFB)
            factor = lax.rsqrt(energy + 0.1 * level + 1e-05)
            real, imag = real * factor, imag * factor
            for q in range(4):
                lanes = slice(q * 128, (q + 1) * 128)
                spread[pl.ds(w * 4 + q, part, stride=16), :] = real[:, lanes]
                spread[pl.ds(8 + w * 4 + q, part, stride=16), :] = imag[:, lanes]

        def pack(i, carry):
            tile = spread[pl.ds(pl.multiple_of(i * 256, 256), 256), :].reshape(16, 16, 128)
            white[pl.ds(block + c * part + i * 16, 16)] = tile.astype(jnp.bfloat16)
            return carry

        lax.fori_loop(0, part // 16, pack, 0)
        if c == 0:
            pl.semaphore_wait(barrier, half + has_left.astype(jnp.int32) + has_right.astype(jnp.int32))

        @pl.when(has_left)
        def _():
            halo(c, 0).start()

        @pl.when(has_right)
        def _():
            halo(c, 1).start()

    @pl.when(has_left)
    def _():
        for c in range(CHUNKS):
            halo(c, 0).wait_send()
            halo(c, 1).wait_recv()

    @pl.when(has_right)
    def _():
        for c in range(CHUNKS):
            halo(c, 1).wait_send()
            halo(c, 0).wait_recv()

    def fold_copy(s):
        return pltpu.make_async_remote_copy(
            src_ref=fold_out.at[s - 1],
            dst_ref=fold_in.at[s - 1],
            send_sem=fold_send.at[s - 1],
            recv_sem=fold_recv.at[s - 1],
            device_id=(chan, mate),
            device_id_type=MESH,
        )

    def lag_copy(s):
        return pltpu.make_async_remote_copy(
            src_ref=send.at[s - 1],
            dst_ref=recv.at[s - 1],
            send_sem=lag_send.at[s - 1],
            recv_sem=lag_recv.at[s - 1],
            device_id=(chan, lax.rem(me + 2 * s, n_tm)),
            device_id_type=MESH,
        )

    base = chan * block - block
    upper = lax.broadcasted_iota(jnp.int32, (8, 128), 0) < 4

    def both_windows(first, second):
        return jnp.where(upper, first, second) + pltpu.roll(jnp.where(upper, second, first), 4, 0)

    def pair_block(target, out):
        first = jnp.int32(0)
        for j in range(n_tm):
            first = jnp.where(owner_ref[0, j] == target, j * channels, first)

        def one_channel(i, inner):
            row = first + i
            own = white[block + row].astype(jnp.float32)
            own_real, own_imag = own[:8], own[8:]
            for k in range(0, K, 2):
                real, imag = [], []
                for far_slot in (k, k + 1):
                    far = white[jnp.maximum(rows_ref[far_slot, row] - base, 0)].astype(jnp.float32)
                    far_real, far_imag = far[:8], far[8:]
                    real.append(own_real * far_real + own_imag * far_imag)
                    imag.append(own_real * far_imag - own_imag * far_real)
                at = pl.ds(pl.multiple_of(i * (4 * K) + 4 * k, 8), 8)
                cr[at, :] = both_windows(*real)
                ci[at, :] = both_windows(*imag)
            return inner

        lax.fori_loop(0, channels, one_channel, 0, unroll=4)

        def gathered(ref):
            return jnp.concatenate(
                [
                    ref[pl.ds(q, pairs, stride=4), :].astype(jnp.bfloat16)
                    for q in range(4)
                ],
                axis=1,
            )

        real = gathered(cr)
        even = jnp.dot(real, cos_ref[...], preferred_element_type=jnp.float32)
        odd = jnp.dot(gathered(ci), sin_ref[...], preferred_element_type=jnp.float32)
        out[:pairs, :LAG] = (even[:, :LAG] + even[:, LAG:]).astype(out.dtype)
        out[:pairs, LAG:] = (odd[:, :LAG] + odd[:, LAG:]).astype(out.dtype)
        edge = lax.dot_general(
            last_ref[...], real, (((1,), (1,)), ((), ())), preferred_element_type=jnp.float32
        )
        edge = edge[:8] + edge[8:]
        pieces = [edge[:, q * 256:(q + 1) * 256] for q in range(pairs // 256)]
        out[pairs:, :] = jnp.concatenate(pieces * (2 // len(pieces)), axis=0).astype(out.dtype)

    def step(s, carry):
        target = lax.rem(me + 2 * s, n_tm)
        pair_block(target + 1 - 2 * side, fold_out.at[s - 1])
        fold_copy(s).start()

        @pl.when(s > 1)
        def _():
            fold_copy(s - 1).wait_recv()
            send[s - 2] = (mine[...] + fold_in[s - 2].astype(jnp.float32)).astype(jnp.bfloat16)
            lag_copy(s - 1).start()

        pair_block(target, mine)
        return carry

    lax.fori_loop(1, half + 1, step, 0)
    fold_copy(half).wait_recv()
    for s in range(1, half):
        lag_copy(s).wait_recv()

    sub = lax.broadcasted_iota(jnp.int32, (128, 128), 0)
    lane = lax.broadcasted_iota(jnp.int32, (128, 128), 1)
    flip = jnp.where(sub + lane == LAG, 1.0, 0.0).astype(jnp.float32)

    def summed(rows):
        total = mine[rows, :] + fold_in[half - 1, rows, :].astype(jnp.float32)
        for s in range(1, half):
            total = total + recv[s - 1, rows, :].astype(jnp.float32)
        return total * scale

    edges = summed(slice(pairs, pairs + 16))
    for c in range(pairs // 128):
        total = summed(slice(c * 128, (c + 1) * 128))
        even, odd = total[:, :LAG], total[:, LAG:]
        at = c * 128 // 256 * 8
        edge = jnp.broadcast_to(edges[at:at + 1, c * 128 % 256:c * 128 % 256 + 128], (128, 128)).T
        odd_edge = odd[:, 0:1]
        odd = jnp.where(lane == 0, 0.0, odd)
        left = jnp.dot(
            even + odd, flip, precision=lax.Precision.HIGHEST, preferred_element_type=jnp.float32
        )
        rows = slice(c * 128, (c + 1) * 128)
        out_ref[rows, :LAG] = jnp.where(lane == 0, edge + odd_edge, left)
        out_ref[rows, LAG:2 * LAG] = even - odd
        out_ref[rows, 2 * LAG:] = edge[:, 0:1] - odd_edge

    for s in range(1, half):
        lag_copy(s).wait_send()
    for s in range(1, half + 1):
        fold_copy(s).wait_send()


def shards(n_chan, n_tm, constants, record, partners, block_owner):
    block, windows, samples = record.shape
    pairs = block * K // n_tm
    scale = 1.0 / math.sqrt(windows * n_tm * NFB)
    smem = pl.BlockSpec(memory_space=pltpu.SMEM)
    vmem = pl.BlockSpec(memory_space=pltpu.VMEM)
    anywhere = pl.BlockSpec(memory_space=pl.ANY)
    return pl.pallas_call(
        functools.partial(kernel, n_chan, n_tm, scale),
        out_shape=jax.ShapeDtypeStruct((pairs, 2 * LAG + 1), jnp.float32),
        in_specs=[smem, smem, anywhere, anywhere, vmem, vmem, vmem],
        out_specs=vmem,
        scratch_shapes=[
            pltpu.VMEM((windows, block, samples), jnp.bfloat16),
            pltpu.VMEM((samples, 2 * NFB), jnp.bfloat16),
            pltpu.VMEM((block // CHUNKS * 16, 128), jnp.float32),
            pltpu.VMEM((3 * block, 16, 128), jnp.bfloat16),
            pltpu.VMEM((pairs * 4, 128), jnp.float32),
            pltpu.VMEM((pairs * 4, 128), jnp.float32),
            pltpu.VMEM((pairs + 16, 2 * LAG), jnp.float32),
            pltpu.VMEM((n_tm // 2, pairs + 16, 2 * LAG), jnp.bfloat16),
            pltpu.VMEM((n_tm // 2, pairs + 16, 2 * LAG), jnp.bfloat16),
            pltpu.VMEM((n_tm // 2 - 1, pairs + 16, 2 * LAG), jnp.bfloat16),
            pltpu.VMEM((n_tm // 2 - 1, pairs + 16, 2 * LAG), jnp.bfloat16),
            pltpu.SemaphoreType.DMA((CHUNKS + 1,)),
            pltpu.SemaphoreType.DMA((2, CHUNKS)),
            pltpu.SemaphoreType.DMA((2, CHUNKS)),
            pltpu.SemaphoreType.DMA((n_tm // 2,)),
            pltpu.SemaphoreType.DMA((n_tm // 2,)),
            pltpu.SemaphoreType.DMA((n_tm // 2 - 1,)),
            pltpu.SemaphoreType.DMA((n_tm // 2 - 1,)),
        ],
        compiler_params=pltpu.CompilerParams(
            collective_id=0, has_side_effects=True, vmem_limit_bytes=52 * 1024 * 1024
        ),
        cost_estimate=pl.CostEstimate(
            flops=2 * block * windows * samples * 2 * NFB, bytes_accessed=16 * 1024 * 1024, transcendentals=0
        ),
    )(jnp.transpose(partners), block_owner, jnp.transpose(record, (1, 0, 2)), *(jnp.asarray(c) for c in constants))


def solution(mesh):
    placed = (P("chan", "tm", None), P("chan", None), P("chan", None))

    def run(record, partners, block_owner):
        body = functools.partial(shards, mesh.shape["chan"], mesh.shape["tm"], tables(record.shape[2]))
        return jax.shard_map(
            body, mesh=mesh, in_specs=placed, out_specs=P(("chan", "tm"), None), check_vma=False
        )(record, partners, block_owner)

    return run
```

```python
import functools
import math

import jax
import jax.numpy as jnp
import ml_dtypes
import numpy as np
from jax import lax
from jax.experimental import pallas as pl
from jax.experimental.pallas import tpu as pltpu
from jax.sharding import PartitionSpec as P

NFB = 512
F0 = 64
K = 8
LAG = 128
CHUNKS = 4
GAIN = 1.45
MESH = pl.DeviceIdType.MESH


def split(table):
    high = table.astype(ml_dtypes.bfloat16)
    low = (table - high.astype(np.float64)).astype(ml_dtypes.bfloat16)
    return high, low


def tables(samples):
    freqs = F0 + np.arange(NFB, dtype=np.int64)
    turn = 2.0 * math.pi / (2 * samples)
    angle = np.arange(samples, dtype=np.int64)[:, None] * freqs[None, :] % (2 * samples) * turn
    fourier = np.concatenate([np.cos(angle), -np.sin(angle)], axis=1).astype(ml_dtypes.bfloat16)
    shift = np.arange(LAG + 1, dtype=np.int64)[None, :]
    phi = freqs[:, None] * shift % (2 * samples) * turn
    cos_high, cos_low = split(GAIN * np.cos(phi))
    sin_high, sin_low = split(GAIN * np.sin(phi))
    cosine = np.concatenate([cos_high[:, :LAG], cos_low[:, :LAG]], axis=1)
    order = np.concatenate([[LAG], np.arange(1, LAG)])
    sine = np.concatenate([sin_high[:, order], sin_low[:, order]], axis=1)
    last = np.concatenate([np.tile(cos_high[:, LAG], (8, 1)), np.tile(cos_low[:, LAG], (8, 1))])
    return fourier, cosine, sine, last


def kernel(n_chan, n_tm, scale, rows_ref, owner_ref, x_hbm, f_hbm, cos_ref, sin_ref, last_ref, out_ref,
           x, table, spread, white, cr, ci, mine, fold_out, fold_in, send, recv,
           load_sem, halo_send, halo_recv, fold_send, fold_recv, lag_send, lag_recv):
    windows, block, samples = x.shape
    chan, me = lax.axis_index("chan"), lax.axis_index("tm")
    half = n_tm // 2
    side = lax.rem(me, 2)
    mate = me + 1 - 2 * side
    has_left, has_right = chan > 0, chan < n_chan - 1
    part = block // CHUNKS
    pairs = out_ref.shape[0]
    channels = pairs // K

    table_copy = pltpu.make_async_copy(f_hbm, table, load_sem.at[CHUNKS])
    loads = [
        pltpu.make_async_copy(
            x_hbm.at[:, pl.ds(c * part, part), :], x.at[:, pl.ds(c * part, part), :], load_sem.at[c]
        )
        for c in range(CHUNKS)
    ]
    loads[0].start()
    table_copy.start()
    for c in range(1, CHUNKS):
        loads[c].start()

    barrier = pltpu.get_barrier_semaphore()
    pl.semaphore_signal(barrier, inc=1, device_id=(chan, mate), device_id_type=MESH)
    for s in range(1, half):
        pl.semaphore_signal(barrier, inc=1, device_id=(chan, lax.rem(me + 2 * s, n_tm)), device_id_type=MESH)

    @pl.when(has_left)
    def _():
        pl.semaphore_signal(barrier, inc=1, device_id=(chan - 1, me), device_id_type=MESH)

    @pl.when(has_right)
    def _():
        pl.semaphore_signal(barrier, inc=1, device_id=(chan + 1, me), device_id_type=MESH)

    def halo(c, way):
        start = 2 * block if way == 0 else 0
        return pltpu.make_async_remote_copy(
            src_ref=white.at[pl.ds(block + c * part, part)],
            dst_ref=white.at[pl.ds(start + c * part, part)],
            send_sem=halo_send.at[way, c],
            recv_sem=halo_recv.at[way, c],
            device_id=(chan - 1 if way == 0 else chan + 1, me),
            device_id_type=MESH,
        )

    for c in range(CHUNKS):
        loads[c].wait()
        if c == 0:
            table_copy.wait()
        for w in range(windows):
            spectra = jnp.dot(x[w, c * part:(c + 1) * part, :], table[...], preferred_element_type=jnp.float32)
            real, imag = spectra[:, :NFB], spectra[:, NFB:]
            energy = real * real + imag * imag
            level = jnp.sum(energy, axis=1, keepdims=True) * (1.0 / NFB)
            factor = lax.rsqrt(energy + 0.1 * level + 1e-05)
            real, imag = real * factor, imag * factor
            for q in range(4):
                lanes = slice(q * 128, (q + 1) * 128)
                spread[pl.ds(w * 4 + q, part, stride=16), :] = real[:, lanes]
                spread[pl.ds(8 + w * 4 + q, part, stride=16), :] = imag[:, lanes]

        def pack(i, carry):
            tile = spread[pl.ds(pl.multiple_of(i * 256, 256), 256), :].reshape(16, 16, 128)
            white[pl.ds(block + c * part + i * 16, 16)] = tile.astype(jnp.bfloat16)
            return carry

        lax.fori_loop(0, part // 16, pack, 0)
        if c == 0:
            pl.semaphore_wait(barrier, half + has_left.astype(jnp.int32) + has_right.astype(jnp.int32))

        @pl.when(has_left)
        def _():
            halo(c, 0).start()

        @pl.when(has_right)
        def _():
            halo(c, 1).start()

    @pl.when(has_left)
    def _():
        for c in range(CHUNKS):
            halo(c, 0).wait_send()
            halo(c, 1).wait_recv()

    @pl.when(has_right)
    def _():
        for c in range(CHUNKS):
            halo(c, 1).wait_send()
            halo(c, 0).wait_recv()

    def fold_copy(s):
        return pltpu.make_async_remote_copy(
            src_ref=fold_out.at[s - 1],
            dst_ref=fold_in.at[s - 1],
            send_sem=fold_send.at[s - 1],
            recv_sem=fold_recv.at[s - 1],
            device_id=(chan, mate),
            device_id_type=MESH,
        )

    def lag_copy(s):
        return pltpu.make_async_remote_copy(
            src_ref=send.at[s - 1],
            dst_ref=recv.at[s - 1],
            send_sem=lag_send.at[s - 1],
            recv_sem=lag_recv.at[s - 1],
            device_id=(chan, lax.rem(me + 2 * s, n_tm)),
            device_id_type=MESH,
        )

    base = chan * block - block
    upper = lax.broadcasted_iota(jnp.int32, (8, 128), 0) < 4

    def both_windows(first, second):
        return jnp.where(upper, first, second) + pltpu.roll(jnp.where(upper, second, first), 4, 0)

    def pair_block(target, out):
        first = jnp.int32(0)
        for j in range(n_tm):
            first = jnp.where(owner_ref[0, j] == target, j * channels, first)

        def one_channel(i, inner):
            row = first + i
            own = white[block + row].astype(jnp.float32)
            own_real, own_imag = own[:8], own[8:]
            for k in range(0, K, 2):
                real, imag = [], []
                for far_slot in (k, k + 1):
                    far = white[jnp.maximum(rows_ref[far_slot, row] - base, 0)].astype(jnp.float32)
                    far_real, far_imag = far[:8], far[8:]
                    real.append(own_real * far_real + own_imag * far_imag)
                    imag.append(own_real * far_imag - own_imag * far_real)
                at = pl.ds(pl.multiple_of(i * (4 * K) + 4 * k, 8), 8)
                cr[at, :] = both_windows(*real)
                ci[at, :] = both_windows(*imag)
            return inner

        lax.fori_loop(0, channels, one_channel, 0, unroll=4)

        def gathered(ref):
            return jnp.concatenate(
                [
                    ref[pl.ds(q, pairs, stride=4), :].astype(jnp.bfloat16)
                    for q in range(4)
                ],
                axis=1,
            )

        real = gathered(cr)
        even = jnp.dot(real, cos_ref[...], preferred_element_type=jnp.float32)
        odd = jnp.dot(gathered(ci), sin_ref[...], preferred_element_type=jnp.float32)
        out[:pairs, :LAG] = (even[:, :LAG] + even[:, LAG:]).astype(out.dtype)
        out[:pairs, LAG:] = (odd[:, :LAG] + odd[:, LAG:]).astype(out.dtype)
        edge = lax.dot_general(
            last_ref[...], real, (((1,), (1,)), ((), ())), preferred_element_type=jnp.float32
        )
        edge = edge[:8] + edge[8:]
        pieces = [edge[:, q * 256:(q + 1) * 256] for q in range(pairs // 256)]
        out[pairs:, :] = jnp.concatenate(pieces * (2 // len(pieces)), axis=0).astype(out.dtype)

    def step(s, carry):
        target = lax.rem(me + 2 * s, n_tm)
        pair_block(target + 1 - 2 * side, fold_out.at[s - 1])
        fold_copy(s).start()

        @pl.when(s > 1)
        def _():
            fold_copy(s - 1).wait_recv()
            send[s - 2] = (mine[...] + fold_in[s - 2].astype(jnp.float32)).astype(jnp.bfloat16)
            lag_copy(s - 1).start()

        pair_block(target, mine)
        return carry

    lax.fori_loop(1, half + 1, step, 0)
    fold_copy(half).wait_recv()
    for s in range(1, half):
        lag_copy(s).wait_recv()

    sub = lax.broadcasted_iota(jnp.int32, (128, 128), 0)
    lane = lax.broadcasted_iota(jnp.int32, (128, 128), 1)
    flip = jnp.where(sub + lane == LAG, 1.0, 0.0).astype(jnp.float32)

    def summed(rows):
        total = mine[rows, :] + fold_in[half - 1, rows, :].astype(jnp.float32)
        for s in range(1, half):
            total = total + recv[s - 1, rows, :].astype(jnp.float32)
        return total * scale

    edges = summed(slice(pairs, pairs + 16))
    for c in range(pairs // 128):
        total = summed(slice(c * 128, (c + 1) * 128))
        even, odd = total[:, :LAG], total[:, LAG:]
        at = c * 128 // 256 * 8
        edge = jnp.broadcast_to(edges[at:at + 1, c * 128 % 256:c * 128 % 256 + 128], (128, 128)).T
        odd_edge = odd[:, 0:1]
        odd = jnp.where(lane == 0, 0.0, odd)
        left = jnp.dot(
            even + odd, flip, precision=lax.Precision.HIGHEST, preferred_element_type=jnp.float32
        )
        rows = slice(c * 128, (c + 1) * 128)
        out_ref[rows, :LAG] = jnp.where(lane == 0, edge + odd_edge, left)
        out_ref[rows, LAG:2 * LAG] = even - odd
        out_ref[rows, 2 * LAG:] = edge[:, 0:1] - odd_edge

    for s in range(1, half):
        lag_copy(s).wait_send()
    for s in range(1, half + 1):
        fold_copy(s).wait_send()


def shards(n_chan, n_tm, constants, record, partners, block_owner):
    block, windows, samples = record.shape
    pairs = block * K // n_tm
    scale = 1.0 / (GAIN * math.sqrt(windows * n_tm * NFB))
    smem = pl.BlockSpec(memory_space=pltpu.SMEM)
    vmem = pl.BlockSpec(memory_space=pltpu.VMEM)
    anywhere = pl.BlockSpec(memory_space=pl.ANY)
    return pl.pallas_call(
        functools.partial(kernel, n_chan, n_tm, scale),
        out_shape=jax.ShapeDtypeStruct((pairs, 2 * LAG + 1), jnp.float32),
        in_specs=[smem, smem, anywhere, anywhere, vmem, vmem, vmem],
        out_specs=vmem,
        scratch_shapes=[
            pltpu.VMEM((windows, block, samples), jnp.bfloat16),
            pltpu.VMEM((samples, 2 * NFB), jnp.bfloat16),
            pltpu.VMEM((block // CHUNKS * 16, 128), jnp.float32),
            pltpu.VMEM((3 * block, 16, 128), jnp.bfloat16),
            pltpu.VMEM((pairs * 4, 128), jnp.float32),
            pltpu.VMEM((pairs * 4, 128), jnp.float32),
            pltpu.VMEM((pairs + 16, 2 * LAG), jnp.float32),
            pltpu.VMEM((n_tm // 2, pairs + 16, 2 * LAG), jnp.bfloat16),
            pltpu.VMEM((n_tm // 2, pairs + 16, 2 * LAG), jnp.bfloat16),
            pltpu.VMEM((n_tm // 2 - 1, pairs + 16, 2 * LAG), jnp.bfloat16),
            pltpu.VMEM((n_tm // 2 - 1, pairs + 16, 2 * LAG), jnp.bfloat16),
            pltpu.SemaphoreType.DMA((CHUNKS + 1,)),
            pltpu.SemaphoreType.DMA((2, CHUNKS)),
            pltpu.SemaphoreType.DMA((2, CHUNKS)),
            pltpu.SemaphoreType.DMA((n_tm // 2,)),
            pltpu.SemaphoreType.DMA((n_tm // 2,)),
            pltpu.SemaphoreType.DMA((n_tm // 2 - 1,)),
            pltpu.SemaphoreType.DMA((n_tm // 2 - 1,)),
        ],
        compiler_params=pltpu.CompilerParams(
            collective_id=0, has_side_effects=True, vmem_limit_bytes=52 * 1024 * 1024
        ),
        cost_estimate=pl.CostEstimate(
            flops=2 * block * windows * samples * 2 * NFB, bytes_accessed=16 * 1024 * 1024, transcendentals=0
        ),
    )(jnp.transpose(partners), block_owner, jnp.transpose(record, (1, 0, 2)), *(jnp.asarray(c) for c in constants))


def solution(mesh):
    placed = (P("chan", "tm", None), P("chan", None), P("chan", None))

    def run(record, partners, block_owner):
        body = functools.partial(shards, mesh.shape["chan"], mesh.shape["tm"], tables(record.shape[2]))
        return jax.shard_map(
            body, mesh=mesh, in_specs=placed, out_specs=P(("chan", "tm"), None), check_vma=False
        )(record, partners, block_owner)

    return run
```
